32 devices in a mesh: cell: 16 (over z, y, x), col: 2 (over core).
Axes of the slice: x: 2, y: 2, z: 4, core: 2. Of those that a mesh axis runs over, the one named last changes fastest.
Arguments:
- panel_block: float32 [8192, 512], P('cell', 'col'), may hold values from -0.176776695 to 0.176776695, as said below
- trailing: float32 [8192, 1792], P('cell', 'col'), may hold values from -6 to 6
Outputs:
- triangle: float32 [512, 512], replicated
- coupling: float32 [512, 1792], P('cell', 'col')
- projected: float32 [8192, 1792], P('cell', 'col')
The draws below stay inside these ranges and needn't reach their ends.
Inputs may be any that keep to these rules, and one draw needn't show every extreme that they name: `panel_block`: the panel has full column rank.
All inputs are finite; a program needn't handle non-finite values.
Results may differ from the reference program's by a relative error of at most 0.0003.
Values sent between devices are 32-bit elements; how exact they have to be, the bound alone decides.
A program may use at most 64 MiB of HBM per device.

```python
import jax
import jax.numpy as jnp
from jax import lax

B = 512
MROWS = 8192
TRAIL = 1792


def draw_panel_block(key, part):
    key_a = jax.random.fold_in(key, 11)
    key_b = jax.random.fold_in(key, 12)
    base = jax.random.truncated_normal(key_a, -4.0, 4.0, (MROWS, B), jnp.float32)
    mixed = base + 0.45 * jnp.roll(base, 1, axis=1) + 0.3 * jnp.roll(base, 7, axis=1)
    column_scale = jnp.exp(jax.random.uniform(key_b, (1, B), jnp.float32, 0.0, 1.3862944))
    shaped = jnp.clip(mixed * column_scale, -16.0, 16.0)
    return (shaped * (1.0 / MROWS ** 0.5)).astype(jnp.float32)


def steps_of(own_key, dims, shards, smallest, high):
    loudness, own = 1.0, jax.random.fold_in(own_key, 6)
    for position, parts in shards:
        draws = jnp.exp(jax.random.uniform(jax.random.fold_in(own, position), (parts,), jnp.float32, smallest / len(shards), high / len(shards)))
        loudness = loudness * jnp.repeat(draws, dims[position] // parts).reshape([-1 if axis == position else 1 for axis in range(len(dims))])
    return loudness


def bell_draw(key, dims, deviation, most, split=(), held_as=jnp.bfloat16):
    values = deviation * jax.random.normal(key, dims, jnp.float32)
    if split:
        values = values * steps_of(key, dims, split, -0.22, 0.18)
    return jnp.clip(values, -most, most).astype(held_as)


def setup_inputs(seed: int = 0) -> dict:
    arg_keys = jax.random.split(jax.random.key(seed), 3)
    return {
        "panel_block": draw_panel_block(jax.random.fold_in(arg_keys[2], 71), 0),
        "trailing": bell_draw(arg_keys[1], (MROWS, TRAIL), 1.0, 6.0, ((0, 16), (1, 2)), jnp.float32),
    }


def reference(panel_block, trailing):
    highest = lax.Precision.HIGHEST
    gram = lax.dot_general(panel_block.astype(jnp.float32), panel_block.astype(jnp.float32), (((0,), (0,)), ((), ())), precision=highest, preferred_element_type=jnp.float32)
    lower_factor = jnp.linalg.cholesky(gram)
    basis_t = jax.scipy.linalg.solve_triangular(lower_factor, jnp.transpose(panel_block), lower=True)
    coupling = jnp.dot(basis_t.astype(jnp.float32), trailing.astype(jnp.float32), precision=highest, preferred_element_type=jnp.float32)
    projected = trailing - lax.dot_general(basis_t.astype(jnp.float32), coupling.astype(jnp.float32), (((0,), (0,)), ((), ())), precision=highest, preferred_element_type=jnp.float32)
    return (jnp.transpose(lower_factor), coupling, projected)
```

```python
import functools

import jax
import jax.numpy as jnp
from jax import lax
from jax.experimental import pallas as pl
from jax.experimental.pallas import tpu as pltpu
from jax.sharding import PartitionSpec as P

MESH = pl.DeviceIdType.MESH
TILE = 128
PIVOTS = 8


def split2(x):
    high = x.astype(jnp.bfloat16)
    low = (x - high.astype(jnp.float32)).astype(jnp.bfloat16)
    return high, low


def split3(x):
    a = x.astype(jnp.bfloat16).astype(jnp.float32)
    rest = x - a
    b = rest.astype(jnp.bfloat16).astype(jnp.float32)
    c = (rest - b).astype(jnp.bfloat16).astype(jnp.float32)
    return a, b, c


def dot(a, b, dims=((1,), (0,))):
    return lax.dot_general(a, b, (dims, ((), ())), preferred_element_type=jnp.float32)


def dot3(a, b_high, b_low, dims=((1,), (0,))):
    a_high, a_low = split2(a)
    return dot(a_high, b_high, dims) + (dot(a_high, b_low, dims) + dot(a_low, b_high, dims))


def small_factor(corner):
    n = PIVOTS
    full = (n, TILE)
    a = {}
    for j in range(n):
        column = jnp.broadcast_to(corner[:, j : j + 1], full)
        for i in range(j, n):
            a[i, j] = jnp.broadcast_to(column[i : i + 1, :], full)
    low, inv, m = {}, {}, {}
    for j in range(n):
        y = lax.rsqrt(a[j, j])
        inv[j] = y * (1.5 - (0.5 * a[j, j]) * (y * y))
        for i in range(j + 1, n):
            low[i, j] = a[i, j] * inv[j]
        for i in range(j + 1, n):
            for p in range(j + 1, i + 1):
                a[i, p] = a[i, p] - low[i, j] * low[p, j]
        m[j, j] = inv[j]
        for p in range(j):
            total = low[j, p] * m[p, p]
            for q in range(p + 1, j):
                total = total + low[j, q] * m[q, p]
            m[j, p] = -inv[j] * total
    sublane = lax.broadcasted_iota(jnp.int32, full, 0)
    columns = []
    for j in range(n):
        column = jnp.zeros(full, jnp.float32)
        for i in range(j, n):
            column = jnp.where(sublane == i, m[i, j], column)
        columns.append(column)
    return columns


def eliminate_block(x_ref, k):
    size = x_ref.shape[0]
    base = k * TILE
    window = slice(base, base + size + TILE)
    width = size + TILE
    lane = lax.broadcasted_iota(jnp.int32, (PIVOTS, TILE), 1)

    def step(b, carry):
        first = pl.multiple_of(base + b * PIVOTS, PIVOTS)
        rows = x_ref[pl.ds(first, PIVOTS), window]
        corner = pltpu.roll(rows[:, :TILE], lax.rem(TILE - b * PIVOTS, TILE), 1)
        columns = small_factor(corner)
        done = None
        for j in range(PIVOTS):
            spread = jnp.concatenate([columns[j]] * (width // TILE), axis=1)
            term = spread * jnp.broadcast_to(rows[j : j + 1, :], (PIVOTS, width))
            done = term if done is None else done + term
        a, bb, c = split3(done)
        below = lane >= (b + 1) * PIVOTS
        la, lb, lc = (jnp.where(below, part[:, :TILE], 0.0) for part in (a, bb, c))
        left = jnp.concatenate([la, la, lb, la, lc, lb], axis=0).astype(jnp.bfloat16)
        right = jnp.concatenate([a, bb, a, c, a, bb], axis=0).astype(jnp.bfloat16)
        change = dot(left, right, ((0,), (0,)))
        x_ref[base : base + TILE, window] = x_ref[base : base + TILE, window] - change
        x_ref[pl.ds(first, PIVOTS), window] = done
        return carry

    lax.fori_loop(0, TILE // PIVOTS, step, 0)
    for r in range(k + 1, size // TILE):
        left = x_ref[base : base + TILE, r * TILE : (r + 1) * TILE]
        change = lax.dot_general(
            left,
            x_ref[base : base + TILE, window],
            (((0,), (0,)), ((), ())),
            precision=lax.Precision.HIGHEST,
            preferred_element_type=jnp.float32,
        )
        x_ref[r * TILE : (r + 1) * TILE, window] = (
            x_ref[r * TILE : (r + 1) * TILE, window] - change
        )


class Summed:
    def __init__(self, part, full_at, near, acc, far, send, recv, groups, place):
        self.part, self.full_at = part, full_at
        self.near, self.acc, self.far = near, acc, far
        self.send, self.recv = send, recv
        self.inner, self.outer = groups
        self.hi, self.lo, self.col = place
        self.big = part.shape[0] // self.inner
        self.small = self.big // self.outer
        self.copies = [[], [], [], []]

    def start(self, phase, d, src, dst, device):
        copy = pltpu.make_async_remote_copy(
            src_ref=src,
            dst_ref=dst,
            send_sem=self.send.at[phase, d - 1],
            recv_sem=self.recv.at[phase, d - 1],
            device_id=(device, self.col),
            device_id_type=MESH,
        )
        copy.start()
        self.copies[phase].append(copy)

    def rows(self, index, size):
        return pl.ds(pl.multiple_of(index * size, size), size)

    def arrived(self, phase):
        for copy in self.copies[phase]:
            copy.wait_recv()

    def begin(self):
        for d in range(1, self.inner):
            other = lax.rem(self.lo + d, self.inner)
            self.start(0, d, self.part.at[self.rows(other, self.big)], self.near.at[d - 1], self.hi * self.inner + other)

    def second(self):
        self.arrived(0)
        total = self.part[self.rows(self.lo, self.big), :]
        for d in range(self.inner - 1):
            total = total + self.near[d]
        self.acc[...] = total
        for d in range(1, self.outer):
            other = lax.rem(self.hi + d, self.outer)
            self.start(1, d, self.acc.at[self.rows(other, self.small)], self.far.at[d - 1], other * self.inner + self.lo)

    def third(self):
        self.arrived(1)
        total = self.acc[self.rows(self.hi, self.small), :]
        for d in range(self.outer - 1):
            total = total + self.far[d]
        mine = self.full_at(self.rows(self.lo * self.outer + self.hi, self.small))
        mine[...] = total
        for d in range(1, self.outer):
            other = lax.rem(self.hi + d, self.outer)
            self.start(2, d, mine, mine, other * self.inner + self.lo)

    def fourth(self):
        self.arrived(2)
        mine = self.full_at(self.rows(self.lo, self.big))
        for d in range(1, self.inner):
            other = lax.rem(self.lo + d, self.inner)
            self.start(3, d, mine, mine, self.hi * self.inner + other)

    def finish(self):
        self.arrived(3)

    def drain(self):
        for phase in self.copies:
            for copy in phase:
                copy.wait_send()


def kernel(
    cells, cols, inner,
    panel_ref, trail_ref, tri_ref, coup_ref, proj_ref,
    parts, panel, panel_t, gram_part, grams, x, high, low, inv_high, inv_low, basis,
    cross_part, cross, coupling,
    g_near, g_acc, g_far, c_near, c_acc, c_far,
    col_send, col_recv, g_send, g_recv, c_send, c_recv,
):
    outer = cells // inner
    me, col = lax.axis_index("cell"), lax.axis_index("col")
    hi, lo = lax.div(me, inner), lax.rem(me, inner)
    rows, own = panel_ref.shape
    size = x.shape[0]
    tiles = size // TILE

    barrier = pltpu.get_barrier_semaphore()
    for d in range(1, inner):
        pl.semaphore_signal(barrier, inc=1, device_id=(hi * inner + lax.rem(lo + d, inner), col), device_id_type=MESH)
    for d in range(1, outer):
        pl.semaphore_signal(barrier, inc=1, device_id=(lax.rem(hi + d, outer) * inner + lo, col), device_id_type=MESH)
    for d in range(1, cols):
        pl.semaphore_signal(barrier, inc=1, device_id=(me, lax.rem(col + d, cols)), device_id_type=MESH)
    pl.semaphore_wait(barrier, inner + outer + cols - 3)

    def share(phase, src, dst):
        copies = []
        for d in range(1, cols):
            copy = pltpu.make_async_remote_copy(
                src_ref=src,
                dst_ref=dst,
                send_sem=col_send.at[phase, d - 1],
                recv_sem=col_recv.at[phase, d - 1],
                device_id=(me, lax.rem(col + d, cols)),
                device_id_type=MESH,
            )
            copy.start()
            copies.append(copy)
        return copies

    panel_copies = share(0, panel_ref, parts.at[col])
    parts[col] = panel_ref[...]
    t_high, t_low = split2(trail_ref[...])
    high[...] = t_high
    low[...] = t_low
    for copy in panel_copies:
        copy.wait_recv()
    for c in range(cols):
        panel[:, c * own : (c + 1) * own] = parts[c]

    @pl.loop(0, tiles)
    def _(i):
        at = pl.ds(pl.multiple_of(i * TILE, TILE), TILE)
        turned = jnp.transpose(panel[:, at])
        panel_t[at, :] = turned
        gram_part[at, :] = lax.dot_general(
            turned,
            panel_ref[...],
            (((1,), (0,)), ((), ())),
            precision=lax.Precision.HIGHEST,
            preferred_element_type=jnp.float32,
        )

    groups, place = (inner, outer), (hi, lo, col)
    gram_sum = Summed(gram_part, lambda r: grams.at[col, r, :], g_near, g_acc, g_far, g_send, g_recv, groups, place)
    cross_sum = Summed(cross_part, lambda r: cross.at[r, :], c_near, c_acc, c_far, c_send, c_recv, groups, place)
    gram_sum.begin()

    @pl.loop(0, tiles)
    def _(i):
        at = pl.ds(pl.multiple_of(i * TILE, TILE), TILE)
        cross_part[at, :] = dot3(panel_t[at, :], high[...], low[...])

    gram_sum.second()
    gram_sum.third()
    cross_sum.begin()
    gram_sum.fourth()
    row = lax.broadcasted_iota(jnp.int32, (size, size), 0)
    column = lax.broadcasted_iota(jnp.int32, (size, size), 1)
    x[:, size:] = jnp.where(row == column, 1.0, 0.0)
    gram_sum.finish()
    gram_copies = share(1, grams.at[col], grams.at[col])
    for copy in gram_copies:
        copy.wait_recv()
    for c in range(cols):
        x[:, c * own : (c + 1) * own] = grams[c]

    later = [cross_sum.second, cross_sum.third, cross_sum.fourth]
    for k in range(tiles):
        eliminate_block(x, k)
        if later:
            later.pop(0)()
    for call in later:
        call()

    tri_ref[...] = jnp.where(row <= column, x[:, :size], 0.0)
    m_high, m_low = split2(x[:, size:])
    inv_high[...] = m_high
    inv_low[...] = m_low

    @pl.loop(0, rows // TILE)
    def _(i):
        at = pl.ds(pl.multiple_of(i * TILE, TILE), TILE)
        basis[at, :] = dot3(panel[at, :], inv_high[...], inv_low[...], ((1,), (1,)))

    cross_sum.finish()
    c_high, c_low = split2(cross[...])
    high[:size] = c_high
    low[:size] = c_low

    @pl.loop(0, tiles)
    def _(i):
        at = pl.ds(pl.multiple_of(i * TILE, TILE), TILE)
        coupling[at, :] = dot3(x[at, size:], high[:size], low[:size])

    share_rows = size // cells
    coup_ref[...] = coupling[pl.ds(pl.multiple_of(me * share_rows, share_rows), share_rows), :]
    k_high, k_low = split2(coupling[...])
    high[:size] = k_high
    low[:size] = k_low

    @pl.loop(0, rows // TILE)
    def _(i):
        at = pl.ds(pl.multiple_of(i * TILE, TILE), TILE)
        proj_ref[at, :] = trail_ref[at, :] - dot3(basis[at, :], high[:size], low[:size])

    for copy in panel_copies + gram_copies:
        copy.wait_send()
    gram_sum.drain()
    cross_sum.drain()


def on_device(cells, cols, panel_block, trailing):
    rows, own = panel_block.shape
    size = own * cols
    wide = trailing.shape[1]
    inner = 1
    while inner * inner < cells:
        inner *= 2
    outer = cells // inner
    big, small = size // inner, size // cells
    tall = max(rows, size)
    f32, bf16 = jnp.float32, jnp.bfloat16
    vmem = pl.BlockSpec(memory_space=pltpu.VMEM)

    def stages(width):
        return [
            pltpu.VMEM((inner - 1, big, width), f32),
            pltpu.VMEM((big, width), f32),
            pltpu.VMEM((outer - 1, small, width), f32),
        ]

    peers = max(inner, outer) - 1
    triangle, coupling, projected = pl.pallas_call(
        functools.partial(kernel, cells, cols, inner),
        out_shape=[
            jax.ShapeDtypeStruct((size, size), f32),
            jax.ShapeDtypeStruct((small, wide), f32),
            jax.ShapeDtypeStruct((rows, wide), f32),
        ],
        in_specs=[vmem] * 2,
        out_specs=[vmem] * 3,
        scratch_shapes=[
            pltpu.VMEM((cols, rows, own), f32),
            pltpu.VMEM((rows, size), f32),
            pltpu.VMEM((size, rows), f32),
            pltpu.VMEM((size, own), f32),
            pltpu.VMEM((cols, size, own), f32),
            pltpu.VMEM((size, 2 * size), f32),
            pltpu.VMEM((tall, wide), bf16),
            pltpu.VMEM((tall, wide), bf16),
            pltpu.VMEM((size, size), bf16),
            pltpu.VMEM((size, size), bf16),
            pltpu.VMEM((rows, size), f32),
            pltpu.VMEM((size, wide), f32),
            pltpu.VMEM((size, wide), f32),
            pltpu.VMEM((size, wide), f32),
        ]
        + stages(own)
        + stages(wide)
        + [pltpu.SemaphoreType.DMA((2, cols - 1))] * 2
        + [pltpu.SemaphoreType.DMA((4, peers))] * 4,
        compiler_params=pltpu.CompilerParams(
            collective_id=0, has_side_effects=True, vmem_limit_bytes=56 * 2**20
        ),
    )(panel_block, trailing)
    return triangle, coupling, projected


def solution(mesh):
    placed = (P("cell", "col"), P("cell", "col"))
    return jax.shard_map(
        functools.partial(on_device, mesh.shape["cell"], mesh.shape["col"]),
        mesh=mesh,
        in_specs=placed,
        out_specs=(P(), P("cell", "col"), P("cell", "col")),
        check_vma=False,
    )
```

```python
import functools

import jax
import jax.numpy as jnp
from jax import lax
from jax.experimental import pallas as pl
from jax.experimental.pallas import tpu as pltpu
from jax.sharding import PartitionSpec as P

MESH = pl.DeviceIdType.MESH
TILE = 128
PIVOTS = 8


def split2(x):
    high = x.astype(jnp.bfloat16)
    low = (x - high.astype(jnp.float32)).astype(jnp.bfloat16)
    return high, low


def split3(x):
    a = x.astype(jnp.bfloat16).astype(jnp.float32)
    rest = x - a
    b = rest.astype(jnp.bfloat16).astype(jnp.float32)
    c = (rest - b).astype(jnp.bfloat16).astype(jnp.float32)
    return a, b, c


def dot(a, b, dims=((1,), (0,))):
    return lax.dot_general(a, b, (dims, ((), ())), preferred_element_type=jnp.float32)


def dot3(a, b_high, b_low, dims=((1,), (0,))):
    a_high, a_low = split2(a)
    return dot(a_high, b_high, dims) + (dot(a_high, b_low, dims) + dot(a_low, b_high, dims))


def small_factor(corner):
    n = PIVOTS
    full = (n, TILE)
    a = {}
    for j in range(n):
        column = jnp.broadcast_to(corner[:, j : j + 1], full)
        for i in range(j, n):
            a[i, j] = jnp.broadcast_to(column[i : i + 1, :], full)
    low, inv, m = {}, {}, {}
    for j in range(n):
        y = lax.rsqrt(a[j, j])
        inv[j] = y * (1.5 - (0.5 * a[j, j]) * (y * y))
        for i in range(j + 1, n):
            low[i, j] = a[i, j] * inv[j]
        for i in range(j + 1, n):
            for p in range(j + 1, i + 1):
                a[i, p] = a[i, p] - low[i, j] * low[p, j]
        m[j, j] = inv[j]
        for p in range(j):
            total = low[j, p] * m[p, p]
            for q in range(p + 1, j):
                total = total + low[j, q] * m[q, p]
            m[j, p] = -inv[j] * total
    sublane = lax.broadcasted_iota(jnp.int32, full, 0)
    columns = []
    for j in range(n):
        column = jnp.zeros(full, jnp.float32)
        for i in range(j, n):
            column = jnp.where(sublane == i, m[i, j], column)
        columns.append(column)
    return columns


def eliminate_rows(x_ref, k, start, stop):
    size = x_ref.shape[0]
    base = k * TILE
    window = slice(base, base + size + TILE)
    width = size + TILE
    lane = lax.broadcasted_iota(jnp.int32, (PIVOTS, TILE), 1)

    def step(b, carry):
        first = pl.multiple_of(base + b * PIVOTS, PIVOTS)
        rows = x_ref[pl.ds(first, PIVOTS), window]
        corner = pltpu.roll(rows[:, :TILE], lax.rem(TILE - b * PIVOTS, TILE), 1)
        columns = small_factor(corner)
        done = None
        for j in range(PIVOTS):
            spread = jnp.concatenate([columns[j]] * (width // TILE), axis=1)
            term = spread * jnp.broadcast_to(rows[j : j + 1, :], (PIVOTS, width))
            done = term if done is None else done + term
        a, bb, c = split3(done)
        below = lane >= (b + 1) * PIVOTS
        la, lb, lc = (jnp.where(below, part[:, :TILE], 0.0) for part in (a, bb, c))
        left = jnp.concatenate([la, la, lb, la, lc, lb], axis=0).astype(jnp.bfloat16)
        right = jnp.concatenate([a, bb, a, c, a, bb], axis=0).astype(jnp.bfloat16)
        change = dot(left, right, ((0,), (0,)))
        x_ref[base : base + TILE, window] = x_ref[base : base + TILE, window] - change
        x_ref[pl.ds(first, PIVOTS), window] = done
        return carry

    lax.fori_loop(start, stop, step, 0)


def update_below(x_ref, k):
    size = x_ref.shape[0]
    base = k * TILE
    window = slice(base, base + size + TILE)
    for r in range(k + 1, size // TILE):
        left = x_ref[base : base + TILE, r * TILE : (r + 1) * TILE]
        change = lax.dot_general(
            left,
            x_ref[base : base + TILE, window],
            (((0,), (0,)), ((), ())),
            precision=lax.Precision.HIGHEST,
            preferred_element_type=jnp.float32,
        )
        x_ref[r * TILE : (r + 1) * TILE, window] = (
            x_ref[r * TILE : (r + 1) * TILE, window] - change
        )


class Summed:
    def __init__(self, part_at, full_at, scratch, send, recv, counts, place, device, size):
        self.part_at, self.full_at = part_at, full_at
        self.near, self.acc, self.far = scratch
        self.send, self.recv = send, recv
        self.nears, self.fars = counts
        self.n, self.f = place
        self.device = device
        self.big = size // self.nears
        self.small = self.big // self.fars
        self.copies = [[], [], [], []]

    def start(self, phase, d, src, dst, device_id):
        copy = pltpu.make_async_remote_copy(
            src_ref=src,
            dst_ref=dst,
            send_sem=self.send.at[phase, d - 1],
            recv_sem=self.recv.at[phase, d - 1],
            device_id=device_id,
            device_id_type=MESH,
        )
        copy.start()
        self.copies[phase].append(copy)

    def rows(self, index, size):
        return pl.ds(pl.multiple_of(index * size, size), size)

    def arrived(self, phase):
        for copy in self.copies[phase]:
            copy.wait_recv()

    def begin(self):
        for d in range(1, self.nears):
            other = lax.rem(self.n + d, self.nears)
            self.start(0, d, self.part_at(self.rows(other, self.big)), self.near.at[d - 1], self.device(other, self.f))

    def second(self):
        self.arrived(0)
        total = self.part_at(self.rows(self.n, self.big))[...]
        for d in range(self.nears - 1):
            total = total + self.near[d]
        self.acc[...] = total
        for d in range(1, self.fars):
            other = lax.rem(self.f + d, self.fars)
            self.start(1, d, self.acc.at[self.rows(other, self.small)], self.far.at[d - 1], self.device(self.n, other))

    def third(self):
        self.arrived(1)
        total = self.acc[self.rows(self.f, self.small), :]
        for d in range(self.fars - 1):
            total = total + self.far[d]
        mine = self.full_at(self.rows(self.n * self.fars + self.f, self.small))
        mine[...] = total
        for d in range(1, self.fars):
            other = lax.rem(self.f + d, self.fars)
            self.start(2, d, mine, mine, self.device(self.n, other))

    def fourth(self):
        self.arrived(2)
        mine = self.full_at(self.rows(self.n, self.big))
        for d in range(1, self.nears):
            other = lax.rem(self.n + d, self.nears)
            self.start(3, d, mine, mine, self.device(other, self.f))

    def finish(self):
        self.arrived(3)

    def drain(self):
        for phase in self.copies:
            for copy in phase:
                copy.wait_send()


def kernel(
    cells, cols, inner,
    panel_ref, trail_ref, tri_ref, coup_ref, proj_ref,
    parts, panel, panel_t, gram_part, grams, x, high, low, inv_high, inv_low, basis,
    cross_part, cross, coupling,
    g_near, g_acc, g_far, a_near, a_acc, a_far, b_near, b_acc, b_far,
    col_send, col_recv, g_send, g_recv, a_send, a_recv, b_send, b_recv,
):
    outer = cells // inner
    me, col = lax.axis_index("cell"), lax.axis_index("col")
    hi, lo = lax.div(me, inner), lax.rem(me, inner)
    rows, own = panel_ref.shape
    size = x.shape[0]
    tiles = size // TILE

    barrier = pltpu.get_barrier_semaphore()
    for d in range(1, inner):
        pl.semaphore_signal(barrier, inc=1, device_id=(hi * inner + lax.rem(lo + d, inner), col), device_id_type=MESH)
    for d in range(1, outer):
        pl.semaphore_signal(barrier, inc=1, device_id=(lax.rem(hi + d, outer) * inner + lo, col), device_id_type=MESH)
    for d in range(1, cols):
        pl.semaphore_signal(barrier, inc=1, device_id=(me, lax.rem(col + d, cols)), device_id_type=MESH)
    pl.semaphore_wait(barrier, inner + outer + cols - 3)

    def share(phase, src, dst):
        copies = []
        for d in range(1, cols):
            copy = pltpu.make_async_remote_copy(
                src_ref=src,
                dst_ref=dst,
                send_sem=col_send.at[phase, d - 1],
                recv_sem=col_recv.at[phase, d - 1],
                device_id=(me, lax.rem(col + d, cols)),
                device_id_type=MESH,
            )
            copy.start()
            copies.append(copy)
        return copies

    panel_copies = share(0, panel_ref, parts.at[col])
    parts[col] = panel_ref[...]
    t_high, t_low = split2(trail_ref[...])
    high[...] = t_high
    low[...] = t_low
    for copy in panel_copies:
        copy.wait_recv()
    for c in range(cols):
        panel[:, c * own : (c + 1) * own] = parts[c]

    @pl.loop(0, tiles)
    def _(i):
        at = pl.ds(pl.multiple_of(i * TILE, TILE), TILE)
        turned = jnp.transpose(panel[:, at])
        panel_t[at, :] = turned
        gram_part[at, :] = lax.dot_general(
            turned,
            panel_ref[...],
            (((1,), (0,)), ((), ())),
            precision=lax.Precision.HIGHEST,
            preferred_element_type=jnp.float32,
        )

    cut = a_acc.shape[1]

    def by_plane(near, far):
        return far * inner + near, col

    def by_line(near, far):
        return near * inner + far, col

    gram_sum = Summed(
        lambda r: gram_part.at[r, :], lambda r: grams.at[col, r, :],
        (g_near, g_acc, g_far), g_send, g_recv, (inner, outer), (lo, hi), by_plane, size,
    )
    sum_a = Summed(
        lambda r: cross_part.at[r, :cut], lambda r: cross.at[r, :cut],
        (a_near, a_acc, a_far), a_send, a_recv, (inner, outer), (lo, hi), by_plane, size,
    )
    sum_b = Summed(
        lambda r: cross_part.at[r, cut:], lambda r: cross.at[r, cut:],
        (b_near, b_acc, b_far), b_send, b_recv, (outer, inner), (hi, lo), by_line, size,
    )
    gram_sum.begin()

    @pl.loop(0, tiles)
    def _(i):
        at = pl.ds(pl.multiple_of(i * TILE, TILE), TILE)
        cross_part[at, :] = dot3(panel_t[at, :], high[...], low[...])

    sum_a.begin()
    sum_b.begin()
    gram_sum.second()
    gram_sum.third()
    gram_sum.fourth()
    row = lax.broadcasted_iota(jnp.int32, (size, size), 0)
    column = lax.broadcasted_iota(jnp.int32, (size, size), 1)
    x[:, size:] = jnp.where(row == column, 1.0, 0.0)
    gram_sum.finish()
    gram_copies = share(1, grams.at[col], grams.at[col])
    for copy in gram_copies:
        copy.wait_recv()
    for c in range(cols):
        x[:, c * own : (c + 1) * own] = grams[c]

    later = {
        1: (sum_a.second, sum_b.second),
        3: (sum_a.third, sum_b.third),
        5: (sum_a.fourth, sum_b.fourth),
    }
    half = TILE // PIVOTS // 2
    for k in range(tiles):
        for part in range(2):
            eliminate_rows(x, k, part * half, part * half + half)
            if part == 1:
                update_below(x, k)
            for call in later.pop(2 * k + part + 1, ()):
                call()
    for calls in later.values():
        for call in calls:
            call()

    tri_ref[...] = jnp.where(row <= column, x[:, :size], 0.0)
    m_high, m_low = split2(x[:, size:])
    inv_high[...] = m_high
    inv_low[...] = m_low

    @pl.loop(0, rows // TILE)
    def _(i):
        at = pl.ds(pl.multiple_of(i * TILE, TILE), TILE)
        basis[at, :] = dot3(panel[at, :], inv_high[...], inv_low[...], ((1,), (1,)))

    sum_a.finish()
    sum_b.finish()
    c_high, c_low = split2(cross[...])
    high[:size] = c_high
    low[:size] = c_low

    @pl.loop(0, tiles)
    def _(i):
        at = pl.ds(pl.multiple_of(i * TILE, TILE), TILE)
        coupling[at, :] = dot3(x[at, size:], high[:size], low[:size])

    share_rows = size // cells
    coup_ref[...] = coupling[pl.ds(pl.multiple_of(me * share_rows, share_rows), share_rows), :]
    k_high, k_low = split2(coupling[...])
    high[:size] = k_high
    low[:size] = k_low

    @pl.loop(0, rows // TILE)
    def _(i):
        at = pl.ds(pl.multiple_of(i * TILE, TILE), TILE)
        proj_ref[at, :] = trail_ref[at, :] - dot3(basis[at, :], high[:size], low[:size])

    for copy in panel_copies + gram_copies:
        copy.wait_send()
    gram_sum.drain()
    sum_a.drain()
    sum_b.drain()


def on_device(cells, cols, panel_block, trailing):
    rows, own = panel_block.shape
    size = own * cols
    wide = trailing.shape[1]
    inner = 1
    while inner * inner < cells:
        inner *= 2
    outer = cells // inner
    small = size // cells
    tall = max(rows, size)
    f32, bf16 = jnp.float32, jnp.bfloat16
    vmem = pl.BlockSpec(memory_space=pltpu.VMEM)

    def stages(nears, fars, width):
        return [
            pltpu.VMEM((nears - 1, size // nears, width), f32),
            pltpu.VMEM((size // nears, width), f32),
            pltpu.VMEM((fars - 1, small, width), f32),
        ]

    cut = wide - max(1, wide // TILE * 2 // 7) * TILE
    peers = max(inner, outer) - 1
    triangle, coupling, projected = pl.pallas_call(
        functools.partial(kernel, cells, cols, inner),
        out_shape=[
            jax.ShapeDtypeStruct((size, size), f32),
            jax.ShapeDtypeStruct((small, wide), f32),
            jax.ShapeDtypeStruct((rows, wide), f32),
        ],
        in_specs=[vmem] * 2,
        out_specs=[vmem] * 3,
        scratch_shapes=[
            pltpu.VMEM((cols, rows, own), f32),
            pltpu.VMEM((rows, size), f32),
            pltpu.VMEM((size, rows), f32),
            pltpu.VMEM((size, own), f32),
            pltpu.VMEM((cols, size, own), f32),
            pltpu.VMEM((size, 2 * size), f32),
            pltpu.VMEM((tall, wide), bf16),
            pltpu.VMEM((tall, wide), bf16),
            pltpu.VMEM((size, size), bf16),
            pltpu.VMEM((size, size), bf16),
            pltpu.VMEM((rows, size), f32),
            pltpu.VMEM((size, wide), f32),
            pltpu.VMEM((size, wide), f32),
            pltpu.VMEM((size, wide), f32),
        ]
        + stages(inner, outer, own)
        + stages(inner, outer, cut)
        + stages(outer, inner, wide - cut)
        + [pltpu.SemaphoreType.DMA((2, cols - 1))] * 2
        + [pltpu.SemaphoreType.DMA((4, peers))] * 6,
        compiler_params=pltpu.CompilerParams(
            collective_id=0, has_side_effects=True, vmem_limit_bytes=56 * 2**20
        ),
    )(panel_block, trailing)
    return triangle, coupling, projected


def solution(mesh):
    placed = (P("cell", "col"), P("cell", "col"))
    return jax.shard_map(
        functools.partial(on_device, mesh.shape["cell"], mesh.shape["col"]),
        mesh=mesh,
        in_specs=placed,
        out_specs=(P(), P("cell", "col"), P("cell", "col")),
        check_vma=False,
    )
```

```python
import functools

import jax
import jax.numpy as jnp
from jax import lax
from jax.experimental import pallas as pl
from jax.experimental.pallas import tpu as pltpu
from jax.sharding import PartitionSpec as P

MESH = pl.DeviceIdType.MESH
TILE = 128
PIVOTS = 8


def split2(x):
    high = x.astype(jnp.bfloat16)
    low = (x - high.astype(jnp.float32)).astype(jnp.bfloat16)
    return high, low


def split3(x):
    a = x.astype(jnp.bfloat16).astype(jnp.float32)
    rest = x - a
    b = rest.astype(jnp.bfloat16).astype(jnp.float32)
    c = (rest - b).astype(jnp.bfloat16).astype(jnp.float32)
    return a, b, c


def dot(a, b, dims=((1,), (0,))):
    return lax.dot_general(a, b, (dims, ((), ())), preferred_element_type=jnp.float32)


def dot3(a, b_high, b_low, dims=((1,), (0,))):
    a_high, a_low = split2(a)
    return dot(a_high, b_high, dims) + (dot(a_high, b_low, dims) + dot(a_low, b_high, dims))


def small_factor(corner):
    n = PIVOTS
    full = (n, TILE)
    a = {}
    for j in range(n):
        column = jnp.broadcast_to(corner[:, j : j + 1], full)
        for i in range(j, n):
            a[i, j] = jnp.broadcast_to(column[i : i + 1, :], full)
    low, inv, m = {}, {}, {}
    for j in range(n):
        y = lax.rsqrt(a[j, j])
        inv[j] = y * (1.5 - (0.5 * a[j, j]) * (y * y))
        for i in range(j + 1, n):
            low[i, j] = a[i, j] * inv[j]
        for i in range(j + 1, n):
            for p in range(j + 1, i + 1):
                a[i, p] = a[i, p] - low[i, j] * low[p, j]
        m[j, j] = inv[j]
        for p in range(j):
            total = low[j, p] * m[p, p]
            for q in range(p + 1, j):
                total = total + low[j, q] * m[q, p]
            m[j, p] = -inv[j] * total
    sublane = lax.broadcasted_iota(jnp.int32, full, 0)
    columns = []
    for j in range(n):
        column = jnp.zeros(full, jnp.float32)
        for i in range(j, n):
            column = jnp.where(sublane == i, m[i, j], column)
        columns.append(column)
    return columns


def eliminate_rows(x_ref, k, start, stop):
    size = x_ref.shape[0]
    base = k * TILE
    window = slice(base, base + size + TILE)
    width = size + TILE
    lane = lax.broadcasted_iota(jnp.int32, (PIVOTS, TILE), 1)

    def step(b, carry):
        first = pl.multiple_of(base + b * PIVOTS, PIVOTS)
        rows = x_ref[pl.ds(first, PIVOTS), window]
        corner = pltpu.roll(rows[:, :TILE], lax.rem(TILE - b * PIVOTS, TILE), 1)
        columns = small_factor(corner)
        done = None
        for j in range(PIVOTS):
            spread = jnp.concatenate([columns[j]] * (width // TILE), axis=1)
            term = spread * jnp.broadcast_to(rows[j : j + 1, :], (PIVOTS, width))
            done = term if done is None else done + term
        a, bb, c = split3(done)
        below = lane >= (b + 1) * PIVOTS
        la, lb, lc = (jnp.where(below, part[:, :TILE], 0.0) for part in (a, bb, c))
        left = jnp.concatenate([la, la, lb, la, lc, lb], axis=0).astype(jnp.bfloat16)
        right = jnp.concatenate([a, bb, a, c, a, bb], axis=0).astype(jnp.bfloat16)
        change = dot(left, right, ((0,), (0,)))
        x_ref[base : base + TILE, window] = x_ref[base : base + TILE, window] - change
        x_ref[pl.ds(first, PIVOTS), window] = done
        return carry

    lax.fori_loop(start, stop, step, 0, unroll=4)


def update_below(x_ref, k):
    size = x_ref.shape[0]
    base = k * TILE
    window = slice(base, base + size + TILE)
    for r in range(k + 1, size // TILE):
        left = x_ref[base : base + TILE, r * TILE : (r + 1) * TILE]
        change = lax.dot_general(
            left,
            x_ref[base : base + TILE, window],
            (((0,), (0,)), ((), ())),
            precision=lax.Precision.HIGHEST,
            preferred_element_type=jnp.float32,
        )
        x_ref[r * TILE : (r + 1) * TILE, window] = (
            x_ref[r * TILE : (r + 1) * TILE, window] - change
        )


class Summed:
    def __init__(self, part_at, full_at, scratch, send, recv, counts, place, device, size):
        self.part_at, self.full_at = part_at, full_at
        self.near, self.acc, self.far = scratch
        self.send, self.recv = send, recv
        self.nears, self.fars = counts
        self.n, self.f = place
        self.device = device
        self.big = size // self.nears
        self.small = self.big // self.fars
        self.copies = [[], [], [], []]

    def start(self, phase, d, src, dst, device_id):
        copy = pltpu.make_async_remote_copy(
            src_ref=src,
            dst_ref=dst,
            send_sem=self.send.at[phase, d - 1],
            recv_sem=self.recv.at[phase, d - 1],
            device_id=device_id,
            device_id_type=MESH,
        )
        copy.start()
        self.copies[phase].append(copy)

    def rows(self, index, size):
        return pl.ds(pl.multiple_of(index * size, size), size)

    def arrived(self, phase):
        for copy in self.copies[phase]:
            copy.wait_recv()

    def begin(self):
        for d in range(1, self.nears):
            other = lax.rem(self.n + d, self.nears)
            self.start(0, d, self.part_at(self.rows(other, self.big)), self.near.at[d - 1], self.device(other, self.f))

    def second(self):
        self.arrived(0)
        total = self.part_at(self.rows(self.n, self.big))[...]
        for d in range(self.nears - 1):
            total = total + self.near[d]
        self.acc[...] = total
        for d in range(1, self.fars):
            other = lax.rem(self.f + d, self.fars)
            self.start(1, d, self.acc.at[self.rows(other, self.small)], self.far.at[d - 1], self.device(self.n, other))

    def third(self):
        self.arrived(1)
        total = self.acc[self.rows(self.f, self.small), :]
        for d in range(self.fars - 1):
            total = total + self.far[d]
        mine = self.full_at(self.rows(self.n * self.fars + self.f, self.small))
        mine[...] = total
        for d in range(1, self.fars):
            other = lax.rem(self.f + d, self.fars)
            self.start(2, d, mine, mine, self.device(self.n, other))

    def fourth(self):
        self.arrived(2)
        mine = self.full_at(self.rows(self.n, self.big))
        for d in range(1, self.nears):
            other = lax.rem(self.n + d, self.nears)
            self.start(3, d, mine, mine, self.device(other, self.f))

    def finish(self):
        self.arrived(3)

    def drain(self):
        for phase in self.copies:
            for copy in phase:
                copy.wait_send()


def kernel(
    cells, cols, inner,
    panel_ref, trail_ref, tri_ref, coup_ref, proj_ref,
    parts, panel, panel_t, gram_part, grams, x, high, low, inv_high, inv_low, basis,
    cross_part, cross, coupling,
    g_near, g_acc, g_far, a_near, a_acc, a_far, b_near, b_acc, b_far,
    col_send, col_recv, g_send, g_recv, a_send, a_recv, b_send, b_recv,
):
    outer = cells // inner
    me, col = lax.axis_index("cell"), lax.axis_index("col")
    hi, lo = lax.div(me, inner), lax.rem(me, inner)
    rows, own = panel_ref.shape
    size = x.shape[0]
    tiles = size // TILE

    barrier = pltpu.get_barrier_semaphore()
    for d in range(1, inner):
        pl.semaphore_signal(barrier, inc=1, device_id=(hi * inner + lax.rem(lo + d, inner), col), device_id_type=MESH)
    for d in range(1, outer):
        pl.semaphore_signal(barrier, inc=1, device_id=(lax.rem(hi + d, outer) * inner + lo, col), device_id_type=MESH)
    for d in range(1, cols):
        pl.semaphore_signal(barrier, inc=1, device_id=(me, lax.rem(col + d, cols)), device_id_type=MESH)
    pl.semaphore_wait(barrier, inner + outer + cols - 3)

    def share(phase, src, dst):
        copies = []
        for d in range(1, cols):
            copy = pltpu.make_async_remote_copy(
                src_ref=src,
                dst_ref=dst,
                send_sem=col_send.at[phase, d - 1],
                recv_sem=col_recv.at[phase, d - 1],
                device_id=(me, lax.rem(col + d, cols)),
                device_id_type=MESH,
            )
            copy.start()
            copies.append(copy)
        return copies

    panel_copies = share(0, panel_ref, parts.at[col])
    parts[col] = panel_ref[...]
    t_high, t_low = split2(trail_ref[...])
    high[...] = t_high
    low[...] = t_low
    for copy in panel_copies:
        copy.wait_recv()
    for c in range(cols):
        panel[:, c * own : (c + 1) * own] = parts[c]

    @pl.loop(0, tiles)
    def _(i):
        at = pl.ds(pl.multiple_of(i * TILE, TILE), TILE)
        turned = jnp.transpose(panel[:, at])
        panel_t[at, :] = turned
        gram_part[at, :] = lax.dot_general(
            turned,
            panel_ref[...],
            (((1,), (0,)), ((), ())),
            precision=lax.Precision.HIGHEST,
            preferred_element_type=jnp.float32,
        )

    cut = a_acc.shape[1]

    def by_plane(near, far):
        return far * inner + near, col

    def by_line(near, far):
        return near * inner + far, col

    gram_sum = Summed(
        lambda r: gram_part.at[r, :], lambda r: grams.at[col, r, :],
        (g_near, g_acc, g_far), g_send, g_recv, (inner, outer), (lo, hi), by_plane, size,
    )
    sum_a = Summed(
        lambda r: cross_part.at[r, :cut], lambda r: cross.at[r, :cut],
        (a_near, a_acc, a_far), a_send, a_recv, (inner, outer), (lo, hi), by_plane, size,
    )
    sum_b = Summed(
        lambda r: cross_part.at[r, cut:], lambda r: cross.at[r, cut:],
        (b_near, b_acc, b_far), b_send, b_recv, (outer, inner), (hi, lo), by_line, size,
    )
    gram_sum.begin()

    @pl.loop(0, tiles)
    def _(i):
        at = pl.ds(pl.multiple_of(i * TILE, TILE), TILE)
        cross_part[at, :] = dot3(panel_t[at, :], high[...], low[...])

    sum_a.begin()
    sum_b.begin()
    gram_sum.second()
    gram_sum.third()
    gram_sum.fourth()
    row = lax.broadcasted_iota(jnp.int32, (size, size), 0)
    column = lax.broadcasted_iota(jnp.int32, (size, size), 1)
    x[:, size:] = jnp.where(row == column, 1.0, 0.0)
    gram_sum.finish()
    gram_copies = share(1, grams.at[col], grams.at[col])
    for copy in gram_copies:
        copy.wait_recv()
    for c in range(cols):
        x[:, c * own : (c + 1) * own] = grams[c]

    later = {
        1: (sum_a.second, sum_b.second),
        3: (sum_a.third, sum_b.third),
        5: (sum_a.fourth, sum_b.fourth),
    }
    half = TILE // PIVOTS // 2
    for k in range(tiles):
        for part in range(2):
            eliminate_rows(x, k, part * half, part * half + half)
            if part == 1:
                update_below(x, k)
            for call in later.pop(2 * k + part + 1, ()):
                call()
    for calls in later.values():
        for call in calls:
            call()

    tri_ref[...] = jnp.where(row <= column, x[:, :size], 0.0)
    m_high, m_low = split2(x[:, size:])
    inv_high[...] = m_high
    inv_low[...] = m_low

    @pl.loop(0, rows // TILE)
    def _(i):
        at = pl.ds(pl.multiple_of(i * TILE, TILE), TILE)
        basis[at, :] = dot3(panel[at, :], inv_high[...], inv_low[...], ((1,), (1,)))

    sum_a.finish()
    sum_b.finish()
    c_high, c_low = split2(cross[...])
    high[:size] = c_high
    low[:size] = c_low

    @pl.loop(0, tiles)
    def _(i):
        at = pl.ds(pl.multiple_of(i * TILE, TILE), TILE)
        coupling[at, :] = dot3(x[at, size:], high[:size], low[:size])

    share_rows = size // cells
    coup_ref[...] = coupling[pl.ds(pl.multiple_of(me * share_rows, share_rows), share_rows), :]
    k_high, k_low = split2(coupling[...])
    high[:size] = k_high
    low[:size] = k_low

    @pl.loop(0, rows // TILE)
    def _(i):
        at = pl.ds(pl.multiple_of(i * TILE, TILE), TILE)
        proj_ref[at, :] = trail_ref[at, :] - dot3(basis[at, :], high[:size], low[:size])

    for copy in panel_copies + gram_copies:
        copy.wait_send()
    gram_sum.drain()
    sum_a.drain()
    sum_b.drain()


def on_device(cells, cols, panel_block, trailing):
    rows, own = panel_block.shape
    size = own * cols
    wide = trailing.shape[1]
    inner = 1
    while inner * inner < cells:
        inner *= 2
    outer = cells // inner
    small = size // cells
    tall = max(rows, size)
    f32, bf16 = jnp.float32, jnp.bfloat16
    vmem = pl.BlockSpec(memory_space=pltpu.VMEM)

    def stages(nears, fars, width):
        return [
            pltpu.VMEM((nears - 1, size // nears, width), f32),
            pltpu.VMEM((size // nears, width), f32),
            pltpu.VMEM((fars - 1, small, width), f32),
        ]

    cut = wide - max(1, wide // TILE * 2 // 7) * TILE
    peers = max(inner, outer) - 1
    triangle, coupling, projected = pl.pallas_call(
        functools.partial(kernel, cells, cols, inner),
        out_shape=[
            jax.ShapeDtypeStruct((size, size), f32),
            jax.ShapeDtypeStruct((small, wide), f32),
            jax.ShapeDtypeStruct((rows, wide), f32),
        ],
        in_specs=[vmem] * 2,
        out_specs=[vmem] * 3,
        scratch_shapes=[
            pltpu.VMEM((cols, rows, own), f32),
            pltpu.VMEM((rows, size), f32),
            pltpu.VMEM((size, rows), f32),
            pltpu.VMEM((size, own), f32),
            pltpu.VMEM((cols, size, own), f32),
            pltpu.VMEM((size, 2 * size), f32),
            pltpu.VMEM((tall, wide), bf16),
            pltpu.VMEM((tall, wide), bf16),
            pltpu.VMEM((size, size), bf16),
            pltpu.VMEM((size, size), bf16),
            pltpu.VMEM((rows, size), f32),
            pltpu.VMEM((size, wide), f32),
            pltpu.VMEM((size, wide), f32),
            pltpu.VMEM((size, wide), f32),
        ]
        + stages(inner, outer, own)
        + stages(inner, outer, cut)
        + stages(outer, inner, wide - cut)
        + [pltpu.SemaphoreType.DMA((2, cols - 1))] * 2
        + [pltpu.SemaphoreType.DMA((4, peers))] * 6,
        compiler_params=pltpu.CompilerParams(
            collective_id=0, has_side_effects=True, vmem_limit_bytes=56 * 2**20
        ),
    )(panel_block, trailing)
    return triangle, coupling, projected


def solution(mesh):
    placed = (P("cell", "col"), P("cell", "col"))
    return jax.shard_map(
        functools.partial(on_device, mesh.shape["cell"], mesh.shape["col"]),
        mesh=mesh,
        in_specs=placed,
        out_specs=(P(), P("cell", "col"), P("cell", "col")),
        check_vma=False,
    )
```
